32 devices in a mesh: row: 4 (over z), col: 8 (over y, x, core).
Axes of the slice: x: 2, y: 2, z: 4, core: 2. Of those that a mesh axis runs over, the one named last changes fastest.
Arguments:
- covariance: float32 [16384, 16384], P('row', 'col'), may hold values from -6 to 6
- wind_direction: int32 [2, 16384], replicated, may hold values from 0 to 3
- wind_speed: int32 [2, 16384], replicated, may hold values from 0 to 7
- speed_table: float32 [2, 8], replicated, may hold values from 0.05 to 0.4
- diffusivity: float32 [128], replicated, may hold values from 0.005 to 0.05
Outputs:
- predicted_covariance: float32 [16384, 16384], P('row', 'col')
The draws below stay inside these ranges and needn't reach their ends.
All inputs are finite; a program needn't handle non-finite values.
Results may differ from the reference program's by a relative error of at most 0.00002.
Values sent between devices are 32-bit elements; how exact they have to be, the bound alone decides.
No kernel may reach another device: no remote copies, remote signals or barrier semaphores. Data moves between devices by JAX's collectives and lax.ppermute only.
A program may use at most 448 MiB of HBM per device.

```python
import math
import jax
import jax.numpy as jnp
from jax import lax

NLAT = 128
NLON = 128
SUBSTEPS = 2
CLASSES = 8
MESH_POINT_COUNT = 16384


def touch_ends(entries, key, low, largest):
    shape = entries.shape
    spot = [jax.random.randint(jax.random.fold_in(key, axis), (), 0, shape[axis]) for axis in range(len(shape))]
    entries = entries.at[tuple(spot)].set(low)
    longest = shape.index(max(shape))
    spot[longest] = (spot[longest] + 1) % shape[longest]
    return entries.at[tuple(spot)].set(largest)


def block_scale(stream_key, extent, cuts, least, largest):
    gain, own = 1.0, jax.random.fold_in(stream_key, 6)
    for axis_at, blocks in cuts:
        heights = jnp.exp(jax.random.uniform(jax.random.fold_in(own, axis_at), (blocks,), jnp.float32, least / len(cuts), largest / len(cuts)))
        gain = gain * jnp.repeat(heights, extent[axis_at] // blocks).reshape([-1 if axis == axis_at else 1 for axis in range(len(extent))])
    return gain


def bell_draw(key, shape, deviation, reach, split=(), kind=jnp.bfloat16):
    values = jax.random.normal(key, shape, jnp.float32) * deviation
    if len(split) > 0:
        values = block_scale(key, shape, split, -0.22, 0.18) * values
    return jnp.clip(values, min=-reach, max=reach).astype(kind)


def setup_inputs(seed: int = 0) -> dict:
    key_list = jax.random.split(jax.random.key(seed), 6)
    covariance = bell_draw(key_list[0], (MESH_POINT_COUNT, MESH_POINT_COUNT), 1.0, 6.0, ((0, 4), (1, 8)), jnp.float32)
    wind_direction = touch_ends(jax.random.randint(key_list[1], (SUBSTEPS, MESH_POINT_COUNT), 0, 4), jax.random.fold_in(key_list[1], 1), 0, 3).astype(jnp.int32)
    wind_speed = touch_ends(jax.random.randint(key_list[2], (SUBSTEPS, MESH_POINT_COUNT), 0, CLASSES), jax.random.fold_in(key_list[2], 1), 0, CLASSES - 1).astype(jnp.int32)
    speed_table = jnp.clip(jax.random.uniform(key_list[3], (2, CLASSES), jnp.float32, 0.05, 0.4), 0.05, 0.4)
    diffusivity = jnp.clip(jnp.exp(jax.random.uniform(key_list[4], (NLAT,), jnp.float32, math.log(0.005), math.log(0.05))), 0.005, 0.05)
    return dict(covariance=covariance, wind_direction=wind_direction, wind_speed=wind_speed, speed_table=speed_table, diffusivity=diffusivity)


def build_coefficients(wind_direction, wind_speed, speed_table, diffusivity, nlat, nlon):
    substeps = wind_direction.shape[0]
    category_list = speed_table.shape[1]
    onehot = (wind_speed[:, :, None] == jnp.arange(category_list, dtype=jnp.int32)).astype(speed_table.dtype)
    lon_courant = jnp.sum(onehot * speed_table[0], axis=2).reshape(substeps, nlat, nlon)
    lat_courant = jnp.sum(onehot * speed_table[1], axis=2).reshape(substeps, nlat, nlon)
    eastward = (wind_direction % 2 == 0).astype(speed_table.dtype).reshape(substeps, nlat, nlon)
    northward = (wind_direction // 2 == 0).astype(speed_table.dtype).reshape(substeps, nlat, nlon)
    diffusion = diffusivity[None, :, None]
    center = 1.0 - lon_courant - lat_courant - 4.0 * diffusion
    western = lon_courant * eastward + diffusion
    eastern = lon_courant * (1.0 - eastward) + diffusion
    southern = lat_courant * northward + diffusion
    northern = lat_courant * (1.0 - northward) + diffusion
    return jnp.stack([center, western, eastern, southern, northern], axis=1)


def substep(tracer, weights):
    padded = jnp.pad(tracer, ((1, 1), (0, 0), (0, 0)))
    southern = padded[:-2]
    northern = padded[2:]
    return (weights[0] * tracer + weights[1] * jnp.roll(tracer, 1, axis=1)
            + weights[2] * jnp.roll(tracer, -1, axis=1) + weights[3] * southern + weights[4] * northern)


def apply_operator(tracer, weight_table):
    for section_idx in range(weight_table.shape[0]):
        tracer = substep(tracer, weight_table[section_idx])
    return tracer


def reference(covariance, wind_direction, wind_speed, speed_table, diffusivity):
    weight_table = build_coefficients(wind_direction, wind_speed, speed_table, diffusivity, NLAT, NLON)[..., None]
    col_width = MESH_POINT_COUNT // 16

    def first_pass(panel_number):
        column_block = lax.dynamic_slice_in_dim(covariance, panel_number * col_width, col_width, 1)
        moved_block = apply_operator(column_block.reshape(NLAT, NLON, col_width), weight_table)
        return moved_block.reshape(MESH_POINT_COUNT, col_width)

    advected = lax.map(first_pass, jnp.arange(16, dtype=jnp.int32))
    advected = jnp.transpose(advected, (1, 0, 2)).reshape(MESH_POINT_COUNT, MESH_POINT_COUNT)

    def second_pass_rims(panel_number):
        row_block = lax.dynamic_slice_in_dim(advected, panel_number * col_width, col_width, 0)
        moved_block = apply_operator(row_block.T.reshape(NLAT, NLON, col_width), weight_table)
        return moved_block.reshape(MESH_POINT_COUNT, col_width).T

    predicted_covariance = lax.map(second_pass_rims, jnp.arange(16, dtype=jnp.int32))
    return predicted_covariance.reshape(MESH_POINT_COUNT, MESH_POINT_COUNT)
```

```python
import functools

import jax
import jax.numpy as jnp
from jax import lax
from jax.experimental import pallas as pl
from jax.experimental.pallas import tpu as pltpu
from jax.sharding import PartitionSpec as P

NLAT = 128
NLON = 128
LANES = 128
PAD = 8
GROUPS = 2
F32 = jnp.float32
ANY = pl.BlockSpec(memory_space=pl.ANY)


def params(mib=56):
    return pltpu.CompilerParams(vmem_limit_bytes=mib << 20)


def cost(flops, size):
    return pl.CostEstimate(flops=flops, bytes_accessed=size, transcendentals=0)


def weights_kernel(rows, cols, wd, ws, table, diff, wr, wc, s_wd, s_ws, s_k, tile):
    def five(first, count, sub):
        for i in range(count):
            lat = jnp.clip(first + i, 0, NLAT - 1)
            at = pl.ds(pl.multiple_of(lat * NLON, NLON), NLON)
            s_wd[i : i + 1, :] = wd[sub : sub + 1, at]
            s_ws[i : i + 1, :] = ws[sub : sub + 1, at]
            s_k[i : i + 1, :] = jnp.full((1, LANES), diff[lat], F32)
        size = -(-count // 8) * 8
        speed, way, k = s_ws[:size, :], s_wd[:size, :], s_k[:size, :]
        u = v = jnp.zeros((size, LANES), F32)
        for c in range(table.shape[1]):
            u = jnp.where(speed == c, table[0, c], u)
            v = jnp.where(speed == c, table[1, c], v)
        lat = first + lax.broadcasted_iota(jnp.int32, (size, LANES), 0)
        keep = jnp.logical_and(lat >= 0, lat < NLAT)
        east = (way & 1) == 0
        north = way < 2
        out = [
            1.0 - u - v - 4.0 * k,
            jnp.where(east, u, 0.0) + k,
            jnp.where(east, 0.0, u) + k,
            jnp.where(north, v, 0.0) + k,
            jnp.where(north, 0.0, v) + k,
        ]
        return [jnp.where(keep, o, 0.0) for o in out]

    lat_row = lax.axis_index("row") * rows
    lat_col = lax.axis_index("col") * cols
    count = rows + 4
    w = five(lat_row - 3, count, 0) + five(lat_row - 4, count, 1)
    tile[...] = jnp.zeros_like(tile)
    for g in range(wr.shape[0]):
        for k in range(10):
            tile[8 * k : 8 * k + 8, :] = w[k][8 * g : 8 * g + 8, :]
        wr[g] = tile[...].T
    for sub in range(2):
        for k, o in enumerate(five(lat_col - 1, cols + 2, sub)):
            wc[5 * sub + k, : o.shape[0], :] = o


def weights_call(rows, cols, wd, ws, table, diff):
    most = -(-(max(rows, cols) + 4) // 8) * 8
    groups = -(-(rows + 4) // 8)
    smem = pl.BlockSpec(memory_space=pltpu.SMEM)
    vmem = pl.BlockSpec(memory_space=pltpu.VMEM)
    return pl.pallas_call(
        functools.partial(weights_kernel, rows, cols),
        in_specs=[vmem, vmem, smem, smem],
        out_specs=[vmem, vmem],
        out_shape=[
            jax.ShapeDtypeStruct((groups, NLON, LANES), F32),
            jax.ShapeDtypeStruct((10, -(-(cols + 2) // 8) * 8, LANES), F32),
        ],
        scratch_shapes=[
            pltpu.VMEM((most, LANES), jnp.int32),
            pltpu.VMEM((most, LANES), jnp.int32),
            pltpu.VMEM((most, LANES), F32),
            pltpu.VMEM((LANES, LANES), F32),
        ],
        compiler_params=params(),
        cost_estimate=cost(100000, 1 << 20),
    )(wd, ws, table, diff)


def lane_weights(wr, index, row, sub):
    w = wr[index // 8, pl.ds(row, 8), :]
    if isinstance(index, int):
        lane = [8 * (5 * sub + k) + index % 8 for k in range(5)]
    else:
        w = pltpu.roll(w, LANES - lax.rem(index, 8), 1)
        lane = [8 * (5 * sub + k) for k in range(5)]
    return [jnp.broadcast_to(w[:, a : a + 1], (8, LANES)) for a in lane]


def edge_kernel(count, first, wr, a, b, left, right, ga, gb):
    side = pl.program_id(0)
    sub_row = lax.broadcasted_iota(jnp.int32, (8, LANES), 0)

    def around(load, j):
        mid = load(8 * j)
        if j == 0:
            west = jnp.where(sub_row == 0, pltpu.roll(load(120), 1, 0), pltpu.roll(mid, 1, 0))
        else:
            west = load(8 * j - 1)
        if j == 15:
            east = jnp.where(sub_row == 7, pltpu.roll(load(0), 7, 0), pltpu.roll(mid, 7, 0))
        else:
            east = load(8 * j + 1)
        return mid, west, east

    @pl.loop(0, count + 2)
    def _(i):
        base = pl.multiple_of(i * 128, 128)
        for j in range(16):
            w = lane_weights(wr, first + i + 2, 8 * j, 0)
            for f, g in ((a, ga), (b, gb)):
                mid, west, east = around(lambda r: f[pl.ds(base + 128 + r, 8), :], j)
                so, no = f[pl.ds(base + 8 * j, 8), :], f[pl.ds(base + 256 + 8 * j, 8), :]
                g[pl.ds(base + 8 * j, 8), :] = w[0] * mid + w[1] * west + w[2] * east + w[3] * so + w[4] * no

    def second(out):
        @pl.loop(0, count)
        def _(i):
            base = pl.multiple_of(i * 128, 128)
            for j in range(16):
                w = lane_weights(wr, first + i + 4, 8 * j, 1)
                for c, g in enumerate((ga, gb)):
                    mid, west, east = around(lambda r: g[pl.ds(base + 128 + r, 8), :], j)
                    so, no = g[pl.ds(base + 8 * j, 8), :], g[pl.ds(base + 256 + 8 * j, 8), :]
                    out[pl.ds(base + 8 * j, 8), c * LANES : (c + 1) * LANES] = (
                        w[0] * mid + w[1] * west + w[2] * east + w[3] * so + w[4] * no
                    )

    pl.when(side == 0)(lambda: second(left))
    pl.when(side == 1)(lambda: second(right))


def edge_call(cov, wr, first, count, inside=0):
    size, wide = (count + 4) * 128, cov.shape[1]
    start = (first - 2 - inside) * 128
    spec = lambda at: pl.BlockSpec(
        (pl.Element(size), pl.Element(LANES)), lambda side: (start, LANES * (at + side * (wide // LANES - 2)))
    )
    out = jax.ShapeDtypeStruct((count * 128, 2 * LANES), F32)
    return pl.pallas_call(
        functools.partial(edge_kernel, count, first),
        grid=(2,),
        in_specs=[pl.BlockSpec(wr.shape, lambda s: (0, 0, 0)), spec(0), spec(1)],
        out_specs=[pl.BlockSpec(out.shape, lambda s: (0, 0))] * 2,
        out_shape=[out, out],
        scratch_shapes=[pltpu.VMEM(((count + 2) * 128, LANES), F32)] * 2,
        compiler_params=params(),
        cost_estimate=cost(count * 128 * 512 * 18, count * 128 * 512 * 8),
    )(wr, cov, cov)


def roll(x, k):
    return pltpu.roll(x, k, 1)


def one_lat(tiles, slot, mode, index, f_ref, f_base, o_ref, o_base, wr, wc, F, G):
    Fs, F1, F2 = F[slot], F[(slot - 1) % 4], F[(slot - 2) % 4]
    G1, G2, G3 = G[(slot - 1) % 4], G[(slot - 2) % 4], G[(slot - 3) % 4]

    @pl.loop(0, 16 // GROUPS)
    def _(j):
        rs = [pl.multiple_of(j * 8 * GROUPS + 8 * i, 8) for i in range(GROUPS)]
        w0 = [lane_weights(wr, index, r, 0) for r in rs] if mode >= 1 else None
        w1 = [lane_weights(wr, index, r, 1) for r in rs] if mode >= 2 else None

        def first(c):
            out = []
            for i, r in enumerate(rs):
                x = f_ref[pl.ds(f_base + r, 8), c * LANES : (c + 1) * LANES]
                Fs[c, pl.ds(PAD + r, 8), :] = x
                if mode >= 1:
                    w = w0[i]
                    g = (
                        w[0] * F1[c, pl.ds(PAD + r, 8), :]
                        + w[1] * F1[c, pl.ds(PAD - 1 + r, 8), :]
                        + w[2] * F1[c, pl.ds(PAD + 1 + r, 8), :]
                        + w[3] * F2[c, pl.ds(PAD + r, 8), :]
                        + w[4] * x
                    )
                    G1[c, pl.ds(PAD + r, 8), :] = g
                    out.append(g)
            return out

        def second(c):
            g = first(c)
            return [
                w[0] * G2[c, pl.ds(PAD + r, 8), :]
                + w[1] * G2[c, pl.ds(PAD - 1 + r, 8), :]
                + w[2] * G2[c, pl.ds(PAD + 1 + r, 8), :]
                + w[3] * G3[c, pl.ds(PAD + r, 8), :]
                + w[4] * g[i]
                for i, (r, w) in enumerate(zip(rs, w1))
            ]

        def across(sub, c, mid, so, no):
            W = [jnp.broadcast_to(wc[5 * sub + k, c + 1 : c + 2, :], (8, LANES)) for k in range(5)]
            out = []
            for i in range(GROUPS):
                t = None
                if mid is not None:
                    t = W[0] * mid[i] + W[1] * roll(mid[i], 1) + W[2] * roll(mid[i], LANES - 1)
                if so is not None:
                    t = W[3] * so[i] if t is None else t + W[3] * so[i]
                if no is not None:
                    t = W[4] * no[i] if t is None else t + W[4] * no[i]
                out.append(t)
            return out

        if mode < 2:
            for c in range(tiles):
                first(c)
            return
        h, u = {-2: None, -1: None}, {-2: None}
        for c in range(tiles + 2):
            h[c] = second(c) if c < tiles else None
            u[c - 1] = across(0, c - 1, h[c - 1], h[c - 2], h[c])
            if c >= 2:
                o = across(1, c - 2, u[c - 2], u[c - 3], u[c - 1])
                for i, r in enumerate(rs):
                    o_ref[pl.ds(o_base + r, 8), (c - 2) * LANES : (c - 1) * LANES] = o[i]

    for ring in (Fs, G1) if mode >= 1 else (Fs,):
        ring[:, PAD - 1 : PAD, :] = ring[:, PAD + 127 : PAD + 128, :]
        ring[:, PAD + 128 : PAD + 129, :] = ring[:, PAD : PAD + 1, :]


def main_kernel(tiles, wr, wc, f_ref, o_ref, *ring):
    F, G = ring[:4], ring[4:8]
    t = pl.program_id(0)

    def four(modes):
        for q in range(4):
            one_lat(tiles, q, modes[q], 4 * t + q + 2, f_ref, 128 * q, o_ref, 128 * q, wr, wc, F, G)

    pl.when(t == 0)(lambda: four((0, 0, 1, 1)))
    pl.when(t > 0)(lambda: four((2, 2, 2, 2)))


def rings(tiles):
    return [pltpu.VMEM((tiles, 128 + 2 * PAD, LANES), F32)] * 8


def main_call(cov, wr, wc):
    rows, wide = cov.shape[0] // 128, cov.shape[1]
    return pl.pallas_call(
        functools.partial(main_kernel, wide // LANES),
        grid=(rows // 4,),
        in_specs=[
            pl.BlockSpec(wr.shape, lambda s: (0, 0, 0)),
            pl.BlockSpec(wc.shape, lambda s: (0, 0, 0)),
            pl.BlockSpec((512, wide), lambda s: (s, 0)),
        ],
        out_specs=pl.BlockSpec(
            (pl.Element(512), pl.Element(wide)), lambda s: (128 * jnp.maximum(4 * s - 2, 2), 0)
        ),
        out_shape=jax.ShapeDtypeStruct(cov.shape, F32),
        scratch_shapes=rings(wide // LANES),
        compiler_params=params(),
        cost_estimate=cost(cov.size * 36, cov.size * 8),
    )(wr, wc, cov)


def rim_kernel(tiles, rows, wr, wc, before, after, c_ref, _, o_ref, *ring):
    F, G = ring[:4], ring[4:8]
    side = pl.program_id(0)

    def six(refs, index):
        for q, (mode, (ref, base)) in enumerate(zip((0, 0, 1, 1, 2, 2), refs)):
            one_lat(tiles, q % 4, mode, index + q, ref, base, o_ref, 128 * (q - 4), wr, wc, F, G)

    own = [(c_ref, 128 * q) for q in range(4)]
    pl.when(side == 0)(lambda: six([(before, 0), (before, 128)] + own, 0))
    pl.when(side == 1)(lambda: six(own + [(after, 0), (after, 128)], rows - 2))


def rim_call(cov, wr, wc, before, after, out):
    rows, wide = cov.shape[0] // 128, cov.shape[1]
    halo = pl.BlockSpec((256, wide), lambda s: (0, 0))
    return pl.pallas_call(
        functools.partial(rim_kernel, wide // LANES, rows),
        grid=(2,),
        in_specs=[
            pl.BlockSpec(wr.shape, lambda s: (0, 0, 0)),
            pl.BlockSpec(wc.shape, lambda s: (0, 0, 0)),
            halo,
            halo,
            pl.BlockSpec((512, wide), lambda s: (s * (rows // 4 - 1), 0)),
            ANY,
        ],
        out_specs=pl.BlockSpec((256, wide), lambda s: (s * (rows // 2 - 1), 0)),
        out_shape=jax.ShapeDtypeStruct(cov.shape, F32),
        scratch_shapes=rings(wide // LANES),
        input_output_aliases={5: 0},
        compiler_params=params(),
        cost_estimate=cost(cov.size * 4, cov.size),
    )(wr, wc, before, after, cov, out)


def halo_kernel(tiles, wc, low, high, o_in, o_ref):
    side = pl.program_id(0)
    height = o_ref.shape[0]

    def weight(sub, k, lat):
        return jnp.broadcast_to(wc[5 * sub + k, lat + 1 : lat + 2, :], (8, LANES))

    def add(ref, near, far, outer, edge, inner, way, at_edge, at_inner):
        a = [weight(0, k, outer) for k in (0, 1, 2, way)]
        b = weight(0, way, edge)
        d = [weight(1, k, edge) for k in (0, 1, 2, way)]
        e = weight(1, way, inner)

        @pl.loop(0, height // 32)
        def _(i):
            for j in range(4):
                at = pl.ds(pl.multiple_of(i * 32 + 8 * j, 8), 8)
                f1, f2 = ref[at, near : near + LANES], ref[at, far : far + LANES]
                u1 = a[0] * f1 + a[1] * roll(f1, 1) + a[2] * roll(f1, LANES - 1) + a[3] * f2
                u0 = b * f1
                o_ref[at, at_edge : at_edge + LANES] = o_in[at, at_edge : at_edge + LANES] + (
                    d[0] * u0 + d[1] * roll(u0, 1) + d[2] * roll(u0, LANES - 1) + d[3] * u1
                )
                o_ref[at, at_inner : at_inner + LANES] = o_in[at, at_inner : at_inner + LANES] + e * u0

    pl.when(side == 0)(lambda: add(low, LANES, 0, -1, 0, 1, 3, 0, LANES))
    pl.when(side == 1)(lambda: add(high, 0, LANES, tiles, tiles - 1, tiles - 2, 4, LANES, 0))


def halo_call(out, wc, low, high, blocks, height):
    wide = out.shape[1]
    first, step, count = blocks
    last = wide // 256 - 1
    at = pl.BlockSpec((height, 256), lambda s, i: (first + step * i, s * last))
    return pl.pallas_call(
        functools.partial(halo_kernel, wide // LANES),
        grid=(2, count),
        in_specs=[
            pl.BlockSpec(wc.shape, lambda s, i: (0, 0, 0)),
            pl.BlockSpec((height, 256), lambda s, i: (jnp.where(s == 0, i, count - 1), 0)),
            pl.BlockSpec((height, 256), lambda s, i: (jnp.where(s == 1, i, 0), 0)),
            at,
        ],
        out_specs=at,
        out_shape=jax.ShapeDtypeStruct(out.shape, F32),
        input_output_aliases={3: 0},
        compiler_params=params(),
        cost_estimate=cost(count * height * 512 * 10, count * height * 512 * 12),
    )(wc, low, high, out)


def local(cov, wind_direction, wind_speed, speed_table, diffusivity):
    rows, tiles = cov.shape[0] // 128, cov.shape[1] // LANES
    n_row, n_col = lax.axis_size("row"), lax.axis_size("col")
    up = lambda n: [(i, i + 1) for i in range(n - 1)]
    down = lambda n: [(i + 1, i) for i in range(n - 1)]
    before = lax.ppermute(cov[-256:], "row", up(n_row))
    after = lax.ppermute(cov[:256], "row", down(n_row))
    wr, wc = weights_call(rows, tiles, wind_direction, wind_speed, speed_table, diffusivity)
    left, right = edge_call(cov, wr, 2, rows - 4)
    low = lax.ppermute(right, "col", up(n_col))
    high = lax.ppermute(left, "col", down(n_col))
    out = main_call(cov, wr, wc)
    top = jnp.concatenate([before, cov[:512]], axis=0)
    bottom = jnp.concatenate([cov[-512:], after], axis=0)
    tl, tr = edge_call(top, wr, 0, 2, inside=-2)
    bl, br = edge_call(bottom, wr, rows - 2, 2, inside=rows - 4)
    low_c = lax.ppermute(jnp.concatenate([tr, br]), "col", up(n_col))
    high_c = lax.ppermute(jnp.concatenate([tl, bl]), "col", down(n_col))
    out = rim_call(cov, wr, wc, before, after, out)
    out = halo_call(out, wc, low, high, (1, 1, rows // 2 - 2), 256)
    return halo_call(out, wc, low_c, high_c, (0, rows // 2 - 1, 2), 256)


def solution(mesh):
    return jax.shard_map(
        local,
        mesh=mesh,
        in_specs=(P("row", "col"), P(), P(), P(), P()),
        out_specs=P("row", "col"),
        check_vma=False,
    )
```

```python
import functools

import jax
import jax.numpy as jnp
from jax import lax
from jax.experimental import pallas as pl
from jax.experimental.pallas import tpu as pltpu
from jax.sharding import PartitionSpec as P

NLAT = 128
NLON = 128
LANES = 128
PAD = 8
GROUPS = 2
F32 = jnp.float32
ANY = pl.BlockSpec(memory_space=pl.ANY)


def params(mib=56):
    return pltpu.CompilerParams(vmem_limit_bytes=mib << 20)


def cost(flops, size):
    return pl.CostEstimate(flops=flops, bytes_accessed=size, transcendentals=0)


def weights_kernel(rows, cols, wd, ws, table, diff, wr, kr, wc, s_wd, s_ws, s_k, tile):
    def parts(first, count, sub):
        for i in range(count):
            lat = jnp.clip(first + i, 0, NLAT - 1)
            at = pl.ds(pl.multiple_of(lat * NLON, NLON), NLON)
            s_wd[i : i + 1, :] = wd[sub : sub + 1, at]
            s_ws[i : i + 1, :] = ws[sub : sub + 1, at]
            s_k[i : i + 1, :] = jnp.full((1, LANES), diff[lat], F32)
        size = -(-count // 8) * 8
        speed, way, k = s_ws[:size, :], s_wd[:size, :], s_k[:size, :]
        u = v = jnp.zeros((size, LANES), F32)
        for c in range(table.shape[1]):
            u = jnp.where(speed == c, table[0, c], u)
            v = jnp.where(speed == c, table[1, c], v)
        lat = first + lax.broadcasted_iota(jnp.int32, (size, LANES), 0)
        keep = jnp.logical_and(lat >= 0, lat < NLAT)
        u, v, k = (jnp.where(keep, x, 0.0) for x in (u, v, k))
        whole = jnp.where(keep, 1.0 - 4.0 * k, 0.0)
        return jnp.where((way & 1) == 0, u, -u), jnp.where(way < 2, v, -v), k, whole

    lat_row = lax.axis_index("row") * rows
    lat_col = lax.axis_index("col") * cols
    count = rows + 5
    x0, y0, _, _ = parts(lat_row - 3, count, 0)
    x1, y1, k, whole = parts(lat_row - 4, count, 1)
    kr[0, : k.shape[0], :] = k
    kr[1, : k.shape[0], :] = whole
    tile[...] = jnp.zeros_like(tile)
    for g in range(wr.shape[0]):
        n = min(32, k.shape[0] - 32 * g)
        for a, x in enumerate((x0, y0, x1, y1)):
            tile[32 * a : 32 * a + n, :] = x[32 * g : 32 * g + n, :]
        wr[g] = tile[...].T
    for sub in range(2):
        x, y, k, whole = parts(lat_col - 1, cols + 2, sub)
        for a, o in enumerate(five(x, y, k, whole)):
            wc[5 * sub + a, : o.shape[0], :] = o


def five(x, y, k, whole):
    none = jnp.zeros_like(x)
    return (
        whole - jnp.abs(x) - jnp.abs(y),
        jnp.maximum(x, none) + k,
        k - jnp.minimum(x, none),
        jnp.maximum(y, none) + k,
        k - jnp.minimum(y, none),
    )


def weights_call(rows, cols, wd, ws, table, diff):
    most = -(-(max(rows, cols) + 5) // 8) * 8
    groups = -(-(rows + 4) // 32)
    smem = pl.BlockSpec(memory_space=pltpu.SMEM)
    vmem = pl.BlockSpec(memory_space=pltpu.VMEM)
    return pl.pallas_call(
        functools.partial(weights_kernel, rows, cols),
        in_specs=[vmem, vmem, smem, smem],
        out_specs=[vmem, vmem, vmem],
        out_shape=[
            jax.ShapeDtypeStruct((groups, NLON, LANES), F32),
            jax.ShapeDtypeStruct((2, -(-(rows + 5) // 8) * 8, LANES), F32),
            jax.ShapeDtypeStruct((10, -(-(cols + 2) // 8) * 8, LANES), F32),
        ],
        scratch_shapes=[
            pltpu.VMEM((most, LANES), jnp.int32),
            pltpu.VMEM((most, LANES), jnp.int32),
            pltpu.VMEM((most, LANES), F32),
            pltpu.VMEM((LANES, LANES), F32),
        ],
        compiler_params=params(),
        cost_estimate=cost(100000, 1 << 23),
    )(wd, ws, table, diff)


def lane_weights(wr, kr, index, row, sub, height=8):
    w = wr[index // 32, pl.ds(row, height), :]
    if isinstance(index, int):
        lane = [32 * (2 * sub + a) + index % 32 for a in range(2)]
    else:
        w = pltpu.roll(w, LANES - lax.rem(index, 32), 1)
        lane = [32 * (2 * sub + a) for a in range(2)]
    x, y = (jnp.broadcast_to(w[:, a : a + 1], (height, LANES)) for a in lane)
    k, whole = (jnp.broadcast_to(kr[a, pl.ds(index + 1 - sub, 1), :], (height, LANES)) for a in range(2))
    return five(x, y, k, whole)


def lay_out(wr, kr, index, row, W, subs=(0, 1)):
    for sub in subs:
        for k, x in enumerate(lane_weights(wr, kr, index, row, sub)):
            W[5 * sub + k, pl.ds(row, 8), :] = x


def edge_kernel(pieces, runs, n_refs, wr, kr, *refs):
    sources, (left, right), f, g, W, sem = refs[:n_refs], refs[n_refs : n_refs + 2], refs[-11:-7], refs[-7:-3], refs[-3:-1], refs[-1]
    sub_row = lax.broadcasted_iota(jnp.int32, (8, LANES), 0)
    wide = sources[0].shape[1]
    copies = []
    for i, (ref, row, count, place) in enumerate(pieces):
        for c, lane in enumerate((0, LANES, wide - 2 * LANES, wide - LANES)):
            copies.append(
                pltpu.make_async_copy(
                    sources[ref].at[pl.ds(row, count * 128), pl.ds(lane, LANES)],
                    f[c].at[pl.ds(place * 128, count * 128), :],
                    sem.at[4 * i + c],
                )
            )
    for c in copies:
        c.start()
    for c in copies:
        c.wait()

    def around(load, j):
        mid = load(8 * j)
        if j == 0:
            west = jnp.where(sub_row == 0, pltpu.roll(load(120), 1, 0), pltpu.roll(mid, 1, 0))
        else:
            west = load(8 * j - 1)
        if j == 15:
            east = jnp.where(sub_row == 7, pltpu.roll(load(0), 7, 0), pltpu.roll(mid, 7, 0))
        else:
            east = load(8 * j + 1)
        return mid, west, east

    def apply(src, base, index, sub, par, store):
        for j in range(16):
            lay_out(wr, kr, index + 1, 8 * j, W[1 - par], (sub,))
            w = [W[par][5 * sub + k, 8 * j : 8 * j + 8, :] for k in range(5)]
            for c in range(4):
                mid, west, east = around(lambda r: src[c][pl.ds(base + 128 + r, 8), :], j)
                so, no = src[c][pl.ds(base + 8 * j, 8), :], src[c][pl.ds(base + 256 + 8 * j, 8), :]
                store(c, 8 * j, w[0] * mid + w[1] * west + w[2] * east + w[3] * so + w[4] * no)

    def to_g(base, place, first, i, par):
        def store(c, r, x):
            g[c][pl.ds(base + r, 8), :] = x

        apply(f, pl.multiple_of(place * 128 + i * 128, 128), first + i + 2, 0, par, store)

    def to_out(base, first, i, at, par):
        def store(c, r, x):
            out = (left, right)[c // 2]
            out[pl.ds(at + r, 8), (c % 2) * LANES : (c % 2 + 1) * LANES] = x

        apply(g, base, first + i + 4, 1, par, store)

    for place, at, first, count in runs:
        for j in range(16):
            lay_out(wr, kr, first + 2, 8 * j, W[0], (0,))
            lay_out(wr, kr, first + 4, 8 * j, W[0], (1,))

        @pl.loop(0, count // 2 + 1)
        def _(i):
            for par in range(2):
                to_g(pl.multiple_of((2 * i + par) * 128, 128), place, first, 2 * i + par, par)

        @pl.loop(0, count // 2)
        def _(i):
            for par in range(2):
                k = 2 * i + par
                to_out(pl.multiple_of(k * 128, 128), first, k, pl.multiple_of(at * 128 + k * 128, 128), par)


def edge_call(sources, wr, kr, pieces, runs, later=()):
    sources = [*sources, *later]
    size = max(p + c for _, _, c, p in pieces)
    count = sum(r[3] for r in runs)
    out = jax.ShapeDtypeStruct((count * 128, 2 * LANES), F32)
    vmem = pl.BlockSpec(memory_space=pltpu.VMEM)
    return pl.pallas_call(
        functools.partial(edge_kernel, pieces, runs, len(sources)),
        in_specs=[vmem, vmem] + [ANY] * len(sources),
        out_specs=[vmem, vmem],
        out_shape=[out, out],
        scratch_shapes=[pltpu.VMEM((size * 128, LANES), F32)] * 4
        + [pltpu.VMEM((max(r[3] for r in runs) * 128 + 256, LANES), F32)] * 4
        + [pltpu.VMEM((10, 128, LANES), F32)] * 2
        + [pltpu.SemaphoreType.DMA((4 * len(pieces),))],
        compiler_params=params(),
        cost_estimate=cost(count * 128 * 512 * 18, count * 128 * 512 * 8),
    )(wr, kr, *sources)


def roll(x, k):
    return pltpu.roll(x, k, 1)


def one_lat(tiles, slot, mode, index, f_ref, f_base, o_ref, o_base, wr, kr, wc, F, G, W):
    Fs, F1, F2 = F[slot], F[(slot - 1) % 4], F[(slot - 2) % 4]
    G1, G2, G3 = G[(slot - 1) % 4], G[(slot - 2) % 4], G[(slot - 3) % 4]
    here, after = W[slot % 2], W[(slot + 1) % 2]

    @pl.loop(0, 16 // GROUPS)
    def _(j):
        rs = [pl.multiple_of(j * 8 * GROUPS + 8 * i, 8) for i in range(GROUPS)]
        for r in rs:
            lay_out(wr, kr, index + 1, r, after)
        w0 = [[here[k, pl.ds(r, 8), :] for k in range(5)] for r in rs] if mode >= 1 else None
        w1 = [[here[5 + k, pl.ds(r, 8), :] for k in range(5)] for r in rs] if mode >= 2 else None

        def first(c):
            out = []
            for i, r in enumerate(rs):
                x = f_ref[pl.ds(f_base + r, 8), c * LANES : (c + 1) * LANES]
                Fs[c, pl.ds(PAD + r, 8), :] = x
                if mode >= 1:
                    w = w0[i]
                    g = (
                        w[0] * F1[c, pl.ds(PAD + r, 8), :]
                        + w[1] * F1[c, pl.ds(PAD - 1 + r, 8), :]
                        + w[2] * F1[c, pl.ds(PAD + 1 + r, 8), :]
                        + w[3] * F2[c, pl.ds(PAD + r, 8), :]
                        + w[4] * x
                    )
                    G1[c, pl.ds(PAD + r, 8), :] = g
                    out.append(g)
            return out

        def second(c):
            g = first(c)
            return [
                w[0] * G2[c, pl.ds(PAD + r, 8), :]
                + w[1] * G2[c, pl.ds(PAD - 1 + r, 8), :]
                + w[2] * G2[c, pl.ds(PAD + 1 + r, 8), :]
                + w[3] * G3[c, pl.ds(PAD + r, 8), :]
                + w[4] * g[i]
                for i, (r, w) in enumerate(zip(rs, w1))
            ]

        def across(sub, c, mid, so, no):
            W = [jnp.broadcast_to(wc[5 * sub + k, c + 1 : c + 2, :], (8, LANES)) for k in range(5)]
            out = []
            for i in range(GROUPS):
                t = None
                if mid is not None:
                    t = W[0] * mid[i] + W[1] * roll(mid[i], 1) + W[2] * roll(mid[i], LANES - 1)
                if so is not None:
                    t = W[3] * so[i] if t is None else t + W[3] * so[i]
                if no is not None:
                    t = W[4] * no[i] if t is None else t + W[4] * no[i]
                out.append(t)
            return out

        if mode < 2:
            for c in range(tiles):
                first(c)
            return
        h, u = {-2: None, -1: None}, {-2: None}
        for c in range(tiles + 2):
            h[c] = second(c) if c < tiles else None
            u[c - 1] = across(0, c - 1, h[c - 1], h[c - 2], h[c])
            if c >= 2:
                o = across(1, c - 2, u[c - 2], u[c - 3], u[c - 1])
                for i, r in enumerate(rs):
                    o_ref[pl.ds(o_base + r, 8), (c - 2) * LANES : (c - 1) * LANES] = o[i]

    for ring in (Fs, G1) if mode >= 1 else (Fs,):
        ring[:, PAD - 1 : PAD, :] = ring[:, PAD + 127 : PAD + 128, :]
        ring[:, PAD + 128 : PAD + 129, :] = ring[:, PAD : PAD + 1, :]


def main_kernel(tiles, wr, kr, wc, f_ref, o_ref, done, *ring):
    F, G, W = ring[:4], ring[4:8], ring[8:]
    t = pl.program_id(0)

    def four(modes):
        for q in range(4):
            one_lat(tiles, q, modes[q], 4 * t + q + 2, f_ref, 128 * q, o_ref, 128 * q, wr, kr, wc, F, G, W)

    done[...] = jnp.zeros_like(done)
    pl.when(t == 0)(lambda: four((0, 0, 1, 1)))
    pl.when(t > 0)(lambda: four((2, 2, 2, 2)))


def rings(tiles):
    return [pltpu.VMEM((tiles, 128 + 2 * PAD, LANES), F32)] * 8 + [pltpu.VMEM((10, 128, LANES), F32)] * 2


def main_call(cov, wr, kr, wc):
    rows, wide = cov.shape[0] // 128, cov.shape[1]
    return pl.pallas_call(
        functools.partial(main_kernel, wide // LANES),
        grid=(rows // 4,),
        in_specs=[
            *[pl.BlockSpec(w.shape, lambda s: (0, 0, 0)) for w in (wr, kr, wc)],
            pl.BlockSpec((512, wide), lambda s: (s, 0)),
        ],
        out_specs=[
            pl.BlockSpec((pl.Element(512), pl.Element(wide)), lambda s: (128 * jnp.maximum(4 * s - 2, 2), 0)),
            pl.BlockSpec((8, LANES), lambda s: (0, 0)),
        ],
        out_shape=[jax.ShapeDtypeStruct(cov.shape, F32), jax.ShapeDtypeStruct((8, LANES), F32)],
        scratch_shapes=rings(wide // LANES),
        compiler_params=params(),
        cost_estimate=cost(cov.size * 36, cov.size * 8),
    )(wr, kr, wc, cov)


def rim_kernel(tiles, rows, wr, kr, wc, before, after, c_ref, _, o_ref, *ring):
    F, G, W = ring[:4], ring[4:8], ring[8:]
    side = pl.program_id(0)

    def six(refs, index):
        for q, (mode, (ref, base)) in enumerate(zip((0, 0, 1, 1, 2, 2), refs)):
            one_lat(tiles, q % 4, mode, index + q, ref, base, o_ref, 128 * (q - 4), wr, kr, wc, F, G, W)

    own = [(c_ref, 128 * q) for q in range(4)]
    pl.when(side == 0)(lambda: six([(before, 0), (before, 128)] + own, 0))
    pl.when(side == 1)(lambda: six(own + [(after, 0), (after, 128)], rows - 2))


def rim_call(cov, wr, kr, wc, before, after, out):
    rows, wide = cov.shape[0] // 128, cov.shape[1]
    halo = pl.BlockSpec((256, wide), lambda s: (0, 0))
    return pl.pallas_call(
        functools.partial(rim_kernel, wide // LANES, rows),
        grid=(2,),
        in_specs=[
            *[pl.BlockSpec(w.shape, lambda s: (0, 0, 0)) for w in (wr, kr, wc)],
            halo,
            halo,
            pl.BlockSpec((512, wide), lambda s: (s * (rows // 4 - 1), 0)),
            ANY,
        ],
        out_specs=pl.BlockSpec((256, wide), lambda s: (s * (rows // 2 - 1), 0)),
        out_shape=jax.ShapeDtypeStruct(cov.shape, F32),
        scratch_shapes=rings(wide // LANES),
        input_output_aliases={6: 0},
        compiler_params=params(),
        cost_estimate=cost(cov.size * 4, cov.size),
    )(wr, kr, wc, before, after, cov, out)


def halo_kernel(tiles, wc, low, high, o_in, o_ref):
    side = pl.program_id(0)
    height = o_ref.shape[0]

    def weight(sub, k, lat):
        return jnp.broadcast_to(wc[5 * sub + k, lat + 1 : lat + 2, :], (8, LANES))

    def add(ref, near, far, outer, edge, inner, way, at_edge, at_inner):
        a = [weight(0, k, outer) for k in (0, 1, 2, way)]
        b = weight(0, way, edge)
        d = [weight(1, k, edge) for k in (0, 1, 2, way)]
        e = weight(1, way, inner)

        @pl.loop(0, height // 128)
        def _(i):
            for j in range(16):
                at = pl.ds(pl.multiple_of(i * 128 + 8 * j, 8), 8)
                f1, f2 = ref[at, near : near + LANES], ref[at, far : far + LANES]
                u1 = a[0] * f1 + a[1] * roll(f1, 1) + a[2] * roll(f1, LANES - 1) + a[3] * f2
                u0 = b * f1
                o_ref[at, at_edge : at_edge + LANES] = o_in[at, at_edge : at_edge + LANES] + (
                    d[0] * u0 + d[1] * roll(u0, 1) + d[2] * roll(u0, LANES - 1) + d[3] * u1
                )
                o_ref[at, at_inner : at_inner + LANES] = o_in[at, at_inner : at_inner + LANES] + e * u0

    pl.when(side == 0)(lambda: add(low, LANES, 0, -1, 0, 1, 3, 0, LANES))
    pl.when(side == 1)(lambda: add(high, 0, LANES, tiles, tiles - 1, tiles - 2, 4, LANES, 0))


def halo_call(out, wc, low, high, blocks, first, step=None):
    wide = out.shape[1]
    height, count = blocks
    step = step or height
    at = pl.BlockSpec(
        (pl.Element(height), pl.Element(256)), lambda s, i: (128 * (first // 128 + step // 128 * i), 256 * (s * (wide // 256 - 1)))
    )
    return pl.pallas_call(
        functools.partial(halo_kernel, wide // LANES),
        grid=(2, count),
        in_specs=[
            pl.BlockSpec(wc.shape, lambda s, i: (0, 0, 0)),
            pl.BlockSpec((height, 256), lambda s, i: (jnp.where(s == 0, i, count - 1), 0)),
            pl.BlockSpec((height, 256), lambda s, i: (jnp.where(s == 1, i, 0), 0)),
            at,
        ],
        out_specs=at,
        out_shape=jax.ShapeDtypeStruct(out.shape, F32),
        input_output_aliases={3: 0},
        compiler_params=params(),
        cost_estimate=cost(count * height * 512 * 10, count * height * 512 * 12),
    )(wc, low, high, out)


def local(cov, wind_direction, wind_speed, speed_table, diffusivity):
    rows, tiles = cov.shape[0] // 128, cov.shape[1] // LANES
    n_row, n_col = lax.axis_size("row"), lax.axis_size("col")
    up = lambda n: [(i, i + 1) for i in range(n - 1)]
    down = lambda n: [(i + 1, i) for i in range(n - 1)]
    wr, kr, wc = weights_call(rows, tiles, wind_direction, wind_speed, speed_table, diffusivity)
    left, right = edge_call([cov], wr, kr, [(0, 0, rows, 0)], [(0, 0, 2, rows - 4)])
    before = lax.ppermute(cov[-256:], "row", up(n_row))
    after = lax.ppermute(cov[:256], "row", down(n_row))
    low = lax.ppermute(right, "col", up(n_col))
    high = lax.ppermute(left, "col", down(n_col))
    out, done = main_call(cov, wr, kr, wc)
    left, right = edge_call(
        [before, cov, after],
        wr,
        kr,
        [(0, 0, 2, 0), (1, 0, 4, 2), (1, 128 * (rows - 4), 4, 6), (2, 0, 2, 10)],
        [(0, 0, 0, 2), (6, 2, rows - 2, 2)],
        [done],
    )
    low_c = lax.ppermute(right, "col", up(n_col))
    high_c = lax.ppermute(left, "col", down(n_col))
    out = rim_call(cov, wr, kr, wc, before, after, out)
    out = halo_call(out, wc, low, high, (128 * (rows - 4) // 2, 2), 256)
    return halo_call(out, wc, low_c, high_c, (256, 2), 0, 128 * (rows - 2))


def solution(mesh):
    return jax.shard_map(
        local,
        mesh=mesh,
        in_specs=(P("row", "col"), P(), P(), P(), P()),
        out_specs=P("row", "col"),
        check_vma=False,
    )
```

```python
import functools

import jax
import jax.numpy as jnp
from jax import lax
from jax.experimental import pallas as pl
from jax.experimental.pallas import tpu as pltpu
from jax.sharding import PartitionSpec as P

NLAT = 128
NLON = 128
LANES = 128
PAD = 8
GROUPS = 2
F32 = jnp.float32
ANY = pl.BlockSpec(memory_space=pl.ANY)


def params(mib=63):
    return pltpu.CompilerParams(vmem_limit_bytes=mib << 20)


def cost(flops, size):
    return pl.CostEstimate(flops=flops, bytes_accessed=size, transcendentals=0)


def weights_kernel(rows, cols, wd, ws, table, diff, wr, kr, wc, s_wd, s_ws, s_k, tile):
    def parts(first, count, sub):
        for i in range(count):
            lat = jnp.clip(first + i, 0, NLAT - 1)
            at = pl.ds(pl.multiple_of(lat * NLON, NLON), NLON)
            s_wd[i : i + 1, :] = wd[sub : sub + 1, at]
            s_ws[i : i + 1, :] = ws[sub : sub + 1, at]
            s_k[i : i + 1, :] = jnp.full((1, LANES), diff[lat], F32)
        size = -(-count // 8) * 8
        speed, way, k = s_ws[:size, :], s_wd[:size, :], s_k[:size, :]
        u = v = jnp.zeros((size, LANES), F32)
        for c in range(table.shape[1]):
            u = jnp.where(speed == c, table[0, c], u)
            v = jnp.where(speed == c, table[1, c], v)
        lat = first + lax.broadcasted_iota(jnp.int32, (size, LANES), 0)
        keep = jnp.logical_and(lat >= 0, lat < NLAT)
        u, v, k = (jnp.where(keep, x, 0.0) for x in (u, v, k))
        whole = jnp.where(keep, 1.0 - 4.0 * k, 0.0)
        return jnp.where((way & 1) == 0, u, -u), jnp.where(way < 2, v, -v), k, whole

    lat_row = lax.axis_index("row") * rows
    lat_col = lax.axis_index("col") * cols
    count = rows + 5
    x0, y0, _, _ = parts(lat_row - 4, count, 0)
    x1, y1, _, _ = parts(lat_row - 5, count, 1)
    _, _, k, whole = parts(lat_row - 4, count, 1)
    kr[0, : k.shape[0], :] = k
    kr[1, : k.shape[0], :] = whole
    tile[...] = jnp.zeros_like(tile)
    for g in range(wr.shape[0]):
        n = min(32, k.shape[0] - 32 * g)
        for a, x in enumerate((x0, y0, x1, y1)):
            tile[32 * a : 32 * a + n, :] = x[32 * g : 32 * g + n, :]
        wr[g] = tile[...].T
    for sub in range(2):
        x, y, k, whole = parts(lat_col - 1, cols + 2, sub)
        for a, o in enumerate(five(x, y, k, whole)):
            wc[5 * sub + a, : o.shape[0], :] = o


def five(x, y, k, whole):
    none = jnp.zeros_like(x)
    return (
        whole - jnp.abs(x) - jnp.abs(y),
        jnp.maximum(x, none) + k,
        k - jnp.minimum(x, none),
        jnp.maximum(y, none) + k,
        k - jnp.minimum(y, none),
    )


def weights_call(rows, cols, wd, ws, table, diff):
    most = -(-(max(rows, cols) + 5) // 8) * 8
    groups = -(-(rows + 5) // 32)
    smem = pl.BlockSpec(memory_space=pltpu.SMEM)
    vmem = pl.BlockSpec(memory_space=pltpu.VMEM)
    return pl.pallas_call(
        functools.partial(weights_kernel, rows, cols),
        in_specs=[vmem, vmem, smem, smem],
        out_specs=[vmem, vmem, vmem],
        out_shape=[
            jax.ShapeDtypeStruct((groups, NLON, LANES), F32),
            jax.ShapeDtypeStruct((2, -(-(rows + 5) // 8) * 8, LANES), F32),
            jax.ShapeDtypeStruct((10, -(-(cols + 2) // 8) * 8, LANES), F32),
        ],
        scratch_shapes=[
            pltpu.VMEM((most, LANES), jnp.int32),
            pltpu.VMEM((most, LANES), jnp.int32),
            pltpu.VMEM((most, LANES), F32),
            pltpu.VMEM((LANES, LANES), F32),
        ],
        compiler_params=params(),
        cost_estimate=cost(100000, 1 << 23),
    )(wd, ws, table, diff)


def lane_weights(wr, kr, index, row, sub, height=8):
    w = wr[(index + 1) // 32, pl.ds(row, height), :]
    if isinstance(index, int):
        lane = [32 * (2 * sub + a) + (index + 1) % 32 for a in range(2)]
    else:
        w = pltpu.roll(w, LANES - lax.rem(index + 1, 32), 1)
        lane = [32 * (2 * sub + a) for a in range(2)]
    x, y = (jnp.broadcast_to(w[:, a : a + 1], (height, LANES)) for a in lane)
    k, whole = (jnp.broadcast_to(kr[a, pl.ds(index + 1 - sub, 1), :], (height, LANES)) for a in range(2))
    return five(x, y, k, whole)


def lay_out(wr, kr, index, row, W, subs=(0, 1)):
    for sub in subs:
        for k, x in enumerate(lane_weights(wr, kr, index, row, sub)):
            W[5 * sub + k, pl.ds(row, 8), :] = x


def edge_kernel(pieces, runs, waits, n_refs, rims, wr, kr, *refs):
    sources, to = refs[:n_refs], refs[n_refs : n_refs + 2]
    if rims:
        rim_to, rim_vmem, rim_sem, refs = refs[n_refs + 2 : n_refs + 4], refs[-3:-1], refs[-1], refs[:-3]
    (left, right), f, g, W, sem, sent = refs[-14:-12], refs[-12:-8], refs[-8:-4], refs[-4:-2], refs[-2], refs[-1]
    sub_row = lax.broadcasted_iota(jnp.int32, (8, LANES), 0)
    wide = sources[0].shape[1]
    copies = []
    for i, (ref, row, count, place) in enumerate(pieces):
        for c, lane in enumerate((0, LANES, wide - 2 * LANES, wide - LANES)):
            copies.append(
                pltpu.make_async_copy(
                    sources[ref].at[pl.ds(row, count * 128), pl.ds(lane, LANES)],
                    f[c].at[pl.ds(place * 128, count * 128), :],
                    sem.at[4 * i + c],
                )
            )
    for c in copies:
        c.start()
    if rims:
        height = sources[0].shape[0]
        rim_in = [
            pltpu.make_async_copy(sources[0].at[pl.ds(at, 256), :], rim_vmem[i], rim_sem.at[i])
            for i, at in enumerate((0, height - 256))
        ]
        rim_out = [pltpu.make_async_copy(rim_vmem[i], rim_to[i], rim_sem.at[2 + i]) for i in range(2)]
        for c in rim_in:
            c.start()

    def around(load, j):
        mid = load(8 * j)
        if j == 0:
            west = jnp.where(sub_row == 0, pltpu.roll(load(120), 1, 0), pltpu.roll(mid, 1, 0))
        else:
            west = load(8 * j - 1)
        if j == 15:
            east = jnp.where(sub_row == 7, pltpu.roll(load(0), 7, 0), pltpu.roll(mid, 7, 0))
        else:
            east = load(8 * j + 1)
        return mid, west, east

    def apply(src, base, index, sub, par, store):
        for j in range(16):
            lay_out(wr, kr, index + 1, 8 * j, W[1 - par], (sub,))
            w = [W[par][5 * sub + k, 8 * j : 8 * j + 8, :] for k in range(5)]
            for c in range(4):
                mid, west, east = around(lambda r: src[c][pl.ds(base + 128 + r, 8), :], j)
                so, no = src[c][pl.ds(base + 8 * j, 8), :], src[c][pl.ds(base + 256 + 8 * j, 8), :]
                store(c, 8 * j, w[0] * mid + w[1] * west + w[2] * east + w[3] * so + w[4] * no)

    def to_g(base, place, first, i, par):
        def store(c, r, x):
            g[c][pl.ds(base + r, 8), :] = x

        apply(f, pl.multiple_of(place * 128 + i * 128, 128), first + i + 2, 0, par, store)

    def to_out(base, first, i, at, par):
        def store(c, r, x):
            out = (left, right)[c // 2]
            out[pl.ds(at + r, 8), (c % 2) * LANES : (c % 2 + 1) * LANES] = x

        apply(g, base, first + i + 4, 1, par, store)

    out = []
    for run, (place, at, first, count) in enumerate(runs):
        for j in range(16):
            lay_out(wr, kr, first + 2, 8 * j, W[0], (0,))
            lay_out(wr, kr, first + 4, 8 * j, W[0], (1,))
        done = 0
        for chunk, size in enumerate(chunks(count)):
            for p in waits[run][chunk]:
                for c in copies[4 * p : 4 * p + 4]:
                    c.wait()
            g_first = done + 2 if done else 0

            @pl.loop(g_first // 2, (done + size + 2) // 2)
            def _(i):
                for par in range(2):
                    to_g(pl.multiple_of((2 * i + par) * 128, 128), place, first, 2 * i + par, par)

            @pl.loop(done // 2, (done + size) // 2)
            def _(i):
                for par in range(2):
                    k = 2 * i + par
                    to_out(pl.multiple_of(k * 128, 128), first, k, pl.multiple_of(at * 128 + k * 128, 128), par)

            rows = pl.ds((at + done) * 128, size * 128)
            for i, (a, b) in enumerate(((left, to[0]), (right, to[1]))):
                out.append(pltpu.make_async_copy(a.at[rows, :], b.at[rows, :], sent.at[len(out)]))
                out[-1].start()
            done += size
            if rims and chunk == 0:
                for c, d in zip(rim_in, rim_out):
                    c.wait()
                    d.start()
    for c in out + (rim_out if rims else []):
        c.wait()


def chunks(count):
    return [8] * (count // 8) + ([count % 8] if count % 8 else [])


def edge_call(sources, wr, kr, pieces, runs, waits, later=(), rims=False):
    size = max(p + c for _, _, c, p in pieces)
    count = sum(r[3] for r in runs)
    out = jax.ShapeDtypeStruct((count * 128, 2 * LANES), F32)
    vmem = pl.BlockSpec(memory_space=pltpu.VMEM)
    n = sum(len(chunks(r[3])) for r in runs)
    rim = jax.ShapeDtypeStruct((256, sources[0].shape[1]), F32)
    return pl.pallas_call(
        functools.partial(edge_kernel, pieces, runs, waits, len(sources) + len(later), rims),
        in_specs=[vmem, vmem] + [vmem if x.shape[0] == 256 else ANY for x in sources] + [ANY] * len(later),
        out_specs=[ANY] * (4 if rims else 2),
        out_shape=[out, out] + ([rim, rim] if rims else []),
        scratch_shapes=[pltpu.VMEM(out.shape, F32)] * 2
        + [pltpu.VMEM((size * 128, LANES), F32)] * 4
        + [pltpu.VMEM((max(r[3] for r in runs) * 128 + 256, LANES), F32)] * 4
        + [pltpu.VMEM((10, 128, LANES), F32)] * 2
        + [pltpu.SemaphoreType.DMA((4 * len(pieces),)), pltpu.SemaphoreType.DMA((2 * n,))]
        + ([pltpu.VMEM(rim.shape, F32)] * 2 + [pltpu.SemaphoreType.DMA((4,))] if rims else []),
        compiler_params=params(),
        cost_estimate=cost(count * 128 * 512 * 18, count * 128 * 512 * 8),
    )(wr, kr, *sources, *later)


def roll(x, k):
    return pltpu.roll(x, k, 1)


def one_lat(tiles, slot, mode, index, f_ref, f_base, o_ref, o_base, next_weights, kr, wc, F, G, W):
    Fs, F1, F2 = F[slot], F[(slot - 1) % 4], F[(slot - 2) % 4]
    G1, G2, G3 = G[(slot - 1) % 4], G[(slot - 2) % 4], G[(slot - 3) % 4]
    here, after = W[slot % 2], W[(slot + 1) % 2]

    @pl.loop(0, 16 // GROUPS)
    def _(j):
        rs = [pl.multiple_of(j * 8 * GROUPS + 8 * i, 8) for i in range(GROUPS)]
        for r in rs:
            w, lane = next_weights(r)
            for a in range(4):
                after[a, pl.ds(r, 8), :] = jnp.broadcast_to(w[:, 32 * a + lane : 32 * a + lane + 1], (8, LANES))

        def weights(sub):
            k, whole = (jnp.broadcast_to(kr[a, pl.ds(index + 1 - sub, 1), :], (8, LANES)) for a in range(2))
            return [five(here[2 * sub, pl.ds(r, 8), :], here[2 * sub + 1, pl.ds(r, 8), :], k, whole) for r in rs]

        w0 = weights(0) if mode >= 1 else None
        w1 = weights(1) if mode >= 2 else None

        def first(c):
            out = []
            for i, r in enumerate(rs):
                x = f_ref[pl.ds(f_base + r, 8), c * LANES : (c + 1) * LANES]
                Fs[c, pl.ds(PAD + r, 8), :] = x
                if mode >= 1:
                    w = w0[i]
                    g = (
                        w[0] * F1[c, pl.ds(PAD + r, 8), :]
                        + w[1] * F1[c, pl.ds(PAD - 1 + r, 8), :]
                        + w[2] * F1[c, pl.ds(PAD + 1 + r, 8), :]
                        + w[3] * F2[c, pl.ds(PAD + r, 8), :]
                        + w[4] * x
                    )
                    G1[c, pl.ds(PAD + r, 8), :] = g
                    out.append(g)
            return out

        def second(c):
            g = first(c)
            return [
                w[0] * G2[c, pl.ds(PAD + r, 8), :]
                + w[1] * G2[c, pl.ds(PAD - 1 + r, 8), :]
                + w[2] * G2[c, pl.ds(PAD + 1 + r, 8), :]
                + w[3] * G3[c, pl.ds(PAD + r, 8), :]
                + w[4] * g[i]
                for i, (r, w) in enumerate(zip(rs, w1))
            ]

        def across(sub, c, mid, so, no):
            W = [jnp.broadcast_to(wc[5 * sub + k, c + 1 : c + 2, :], (8, LANES)) for k in range(5)]
            out = []
            for i in range(GROUPS):
                t = None
                if mid is not None:
                    t = W[0] * mid[i] + W[1] * roll(mid[i], 1) + W[2] * roll(mid[i], LANES - 1)
                if so is not None:
                    t = W[3] * so[i] if t is None else t + W[3] * so[i]
                if no is not None:
                    t = W[4] * no[i] if t is None else t + W[4] * no[i]
                out.append(t)
            return out

        if mode < 2:
            for c in range(tiles):
                first(c)
            return
        h, u = {-2: None, -1: None}, {-2: None}
        for c in range(tiles + 2):
            h[c] = second(c) if c < tiles else None
            u[c - 1] = across(0, c - 1, h[c - 1], h[c - 2], h[c])
            if c >= 2:
                o = across(1, c - 2, u[c - 2], u[c - 3], u[c - 1])
                for i, r in enumerate(rs):
                    o_ref[pl.ds(o_base + r, 8), (c - 2) * LANES : (c - 1) * LANES] = o[i]

    for ring in (Fs, G1) if mode >= 1 else (Fs,):
        ring[:, PAD - 1 : PAD, :] = ring[:, PAD + 127 : PAD + 128, :]
        ring[:, PAD + 128 : PAD + 129, :] = ring[:, PAD : PAD + 1, :]


def main_kernel(tiles, wr, kr, wc, f_ref, o_ref, done, *ring):
    F, G, W, turned = ring[:4], ring[4:8], ring[8:10], ring[10]
    t = pl.program_id(0)
    turned[...] = pltpu.roll(wr[(4 * t + 4) // 32], LANES - lax.rem(4 * t + 4, 32), 1)

    def four(modes):
        for q in range(4):
            next_weights = lambda r, q=q: (turned[pl.ds(r, 8), :], q)
            one_lat(tiles, q, modes[q], 4 * t + q + 2, f_ref, 128 * q, o_ref, 128 * q, next_weights, kr, wc, F, G, W)

    done[...] = jnp.zeros_like(done)
    pl.when(t == 0)(lambda: four((0, 0, 1, 1)))
    pl.when(t > 0)(lambda: four((2, 2, 2, 2)))


def rings(tiles):
    return [pltpu.VMEM((tiles, 128 + 2 * PAD, LANES), F32)] * 8 + [pltpu.VMEM((4, 128, LANES), F32)] * 2


def main_call(cov, wr, kr, wc):
    rows, wide = cov.shape[0] // 128, cov.shape[1]
    return pl.pallas_call(
        functools.partial(main_kernel, wide // LANES),
        grid=(rows // 4,),
        in_specs=[
            *[pl.BlockSpec(w.shape, lambda s: (0, 0, 0)) for w in (wr, kr, wc)],
            pl.BlockSpec((512, wide), lambda s: (s, 0)),
        ],
        out_specs=[
            pl.BlockSpec((pl.Element(512), pl.Element(wide)), lambda s: (128 * jnp.maximum(4 * s - 2, 2), 0)),
            pl.BlockSpec((8, LANES), lambda s: (0, 0)),
        ],
        out_shape=[jax.ShapeDtypeStruct(cov.shape, F32), jax.ShapeDtypeStruct((8, LANES), F32)],
        scratch_shapes=rings(wide // LANES) + [pltpu.VMEM((128, LANES), F32)],
        compiler_params=params(),
        cost_estimate=cost(cov.size * 36, cov.size * 8),
    )(wr, kr, wc, cov)


def add_halo(tiles, wc, side, halo, e_ref):
    edge, way = (0, 3) if side == 0 else (tiles - 1, 4)
    outer, inner = (-1, 1) if side == 0 else (tiles, tiles - 2)
    near, far = (LANES, 0) if side == 0 else (0, LANES)
    at_edge, at_inner = (0, LANES) if side == 0 else (LANES, 0)

    def weight(sub, k, lat):
        return jnp.broadcast_to(wc[5 * sub + k, lat + 1 : lat + 2, :], (8, LANES))

    a = [weight(0, k, outer) for k in (0, 1, 2, way)]
    b = weight(0, way, edge)
    d = [weight(1, k, edge) for k in (0, 1, 2, way)]
    e = weight(1, way, inner)

    @pl.loop(0, halo.shape[0] // 128)
    def _(i):
        for j in range(16):
            at = pl.ds(pl.multiple_of(i * 128 + 8 * j, 8), 8)
            f1, f2 = halo[at, near : near + LANES], halo[at, far : far + LANES]
            u1 = a[0] * f1 + a[1] * roll(f1, 1) + a[2] * roll(f1, LANES - 1) + a[3] * f2
            u0 = b * f1
            e_ref[at, at_edge : at_edge + LANES] = e_ref[at, at_edge : at_edge + LANES] + (
                d[0] * u0 + d[1] * roll(u0, 1) + d[2] * roll(u0, LANES - 1) + d[3] * u1
            )
            e_ref[at, at_inner : at_inner + LANES] = e_ref[at, at_inner : at_inner + LANES] + e * u0


class Copies:
    def __init__(self, sem):
        self.sem, self.n = sem, 0

    def start(self, src, dst):
        c = pltpu.make_async_copy(src, dst, self.sem.at[self.n])
        self.n += 1
        c.start()
        return c


def tail_kernel(tiles, rows, wr, kr, wc, before, after, low, high, cov, o_in, o_hbm, *scratch):
    halo, own, rim, side_halo, side_own = (scratch[2 * i : 2 * i + 2] for i in range(5))
    F, G, W, sem = scratch[10:14], scratch[14:18], scratch[18:20], scratch[20]
    copies = Copies(sem)
    wide, size = tiles * LANES, (rows - 4) * 128
    inside = pl.ds(256, size)
    lanes = [pl.ds(0, 256), pl.ds(wide - 256, 256)]

    def bring(i):
        if i < 2:
            x = (before, after)[i]
            return [copies.start(x, halo[i]), copies.start(cov.at[pl.ds(i * (rows - 4) * 128, 512), :], own[i])]
        x = (low, high)[i - 2]
        return [copies.start(x, side_halo[i - 2]), copies.start(o_in.at[inside, lanes[i - 2]], side_own[i - 2])]

    ins, out = [bring(0)], []
    for i in range(2):
        for c in ins[i]:
            c.wait()
        ins += [bring(1), bring(2)] if i == 0 else [bring(3)]
        mine, theirs = [(own[i], 128 * q) for q in range(4)], [(halo[i], 128 * q) for q in range(2)]
        index = (rows - 2) * i
        for q, (mode, (ref, base)) in enumerate(zip((0, 0, 1, 1, 2, 2), mine + theirs if i else theirs + mine)):
            at = index + q + 2
            next_weights = lambda r, at=at: (wr[at // 32, pl.ds(r, 8), :], at % 32)
            one_lat(tiles, q % 4, mode, index + q, ref, base, rim[i], 128 * (q - 4), next_weights, kr, wc, F, G, W)
        out.append(copies.start(rim[i], o_hbm.at[pl.ds(i * (rows - 2) * 128, 256), :]))
    for i in range(2):
        for c in ins[2 + i]:
            c.wait()
        add_halo(tiles, wc, i, side_halo[i], side_own[i])
        out.append(copies.start(side_own[i], o_hbm.at[inside, lanes[i]]))
    for c in out:
        c.wait()


def tail_call(cov, wr, kr, wc, before, after, low, high, out):
    rows, wide = cov.shape[0] // 128, cov.shape[1]
    vmem = pl.BlockSpec(memory_space=pltpu.VMEM)
    return pl.pallas_call(
        functools.partial(tail_kernel, wide // LANES, rows),
        in_specs=[vmem] * 3 + [ANY] * 6,
        out_specs=ANY,
        out_shape=jax.ShapeDtypeStruct(cov.shape, F32),
        scratch_shapes=[pltpu.VMEM((256, wide), F32)] * 2
        + [pltpu.VMEM((512, wide), F32)] * 2
        + [pltpu.VMEM((256, wide), F32)] * 2
        + [pltpu.VMEM(low.shape, F32)] * 4
        + rings(wide // LANES)
        + [pltpu.SemaphoreType.DMA((12,))],
        input_output_aliases={8: 0},
        compiler_params=params(),
        cost_estimate=cost(cov.size * 8, cov.size * 3),
    )(wr, kr, wc, before, after, low, high, cov, out)


def corner_kernel(tiles, rows, wc, low, high, o_in, o_hbm, own0, own1, halo0, halo1, sem):
    copies = Copies(sem)
    wide = tiles * LANES
    parts = [(i, pl.ds(256 * i, 256), pl.ds(i * (rows - 2) * 128, 256)) for i in range(2)]
    lanes = [pl.ds(0, 256), pl.ds(wide - 256, 256)]
    own = (own0, own1)
    ins = [[copies.start(o_in.at[there, lanes[s]], own[s].at[here, :]) for _, here, there in parts] for s in range(2)]
    for s, (x, halo) in enumerate(((low, halo0), (high, halo1))):
        ins[s].append(copies.start(x, halo))
    out = []
    for s, halo in enumerate((halo0, halo1)):
        for c in ins[s]:
            c.wait()
        add_halo(tiles, wc, s, halo, own[s])
        out += [copies.start(own[s].at[here, :], o_hbm.at[there, lanes[s]]) for _, here, there in parts]
    for c in out:
        c.wait()


def corner_call(wc, low, high, out):
    rows, wide = out.shape[0] // 128, out.shape[1]
    vmem = pl.BlockSpec(memory_space=pltpu.VMEM)
    return pl.pallas_call(
        functools.partial(corner_kernel, wide // LANES, rows),
        in_specs=[vmem] + [ANY] * 3,
        out_specs=ANY,
        out_shape=jax.ShapeDtypeStruct(out.shape, F32),
        scratch_shapes=[pltpu.VMEM(low.shape, F32)] * 4 + [pltpu.SemaphoreType.DMA((10,))],
        input_output_aliases={3: 0},
        compiler_params=params(),
        cost_estimate=cost(low.size * 20, low.size * 24),
    )(wc, low, high, out)


def local(cov, wind_direction, wind_speed, speed_table, diffusivity):
    rows, tiles = cov.shape[0] // 128, cov.shape[1] // LANES
    n_row, n_col = lax.axis_size("row"), lax.axis_size("col")
    up = lambda n: [(i, i + 1) for i in range(n - 1)]
    down = lambda n: [(i + 1, i) for i in range(n - 1)]
    wr, kr, wc = weights_call(rows, tiles, wind_direction, wind_speed, speed_table, diffusivity)
    sizes = chunks(rows - 4)
    sizes[0] += 4
    starts = [sum(sizes[:i]) for i in range(len(sizes))]
    pieces = [(0, 128 * a, n, a) for a, n in zip(starts, sizes)]
    left, right, first, final = edge_call(
        [cov], wr, kr, pieces, [(0, 0, 2, rows - 4)], [[[i] for i in range(len(sizes))]], rims=True
    )
    before = lax.ppermute(final, "row", up(n_row))
    after = lax.ppermute(first, "row", down(n_row))
    low = lax.ppermute(right, "col", up(n_col))
    high = lax.ppermute(left, "col", down(n_col))
    out, done = main_call(cov, wr, kr, wc)
    left, right = edge_call(
        [before, cov, after],
        wr,
        kr,
        [(0, 0, 2, 0), (1, 0, 4, 2), (1, 128 * (rows - 4), 4, 6), (2, 0, 2, 10)],
        [(0, 0, 0, 2), (6, 2, rows - 2, 2)],
        [[[0, 1]], [[2, 3]]],
        [done],
    )
    low_c = lax.ppermute(right, "col", up(n_col))
    high_c = lax.ppermute(left, "col", down(n_col))
    out = tail_call(cov, wr, kr, wc, before, after, low, high, out)
    return corner_call(wc, low_c, high_c, out)


def solution(mesh):
    return jax.shard_map(
        local,
        mesh=mesh,
        in_specs=(P("row", "col"), P(), P(), P(), P()),
        out_specs=P("row", "col"),
        check_vma=False,
    )
```

```python
import functools

import jax
import jax.numpy as jnp
from jax import lax
from jax.experimental import pallas as pl
from jax.experimental.pallas import tpu as pltpu
from jax.sharding import PartitionSpec as P

NLAT = 128
NLON = 128
LANES = 128
PAD = 8
GROUPS = 16
PART = 2
F32 = jnp.float32
ANY = pl.BlockSpec(memory_space=pl.ANY)


def params(mib=63):
    return pltpu.CompilerParams(vmem_limit_bytes=mib << 20)


def cost(flops, size):
    return pl.CostEstimate(flops=flops, bytes_accessed=size, transcendentals=0)


def weights_kernel(rows, cols, wd, ws, table, diff, wr, kr, wc, s_wd, s_ws, s_k, tile):
    def parts(first, count, sub):
        for i in range(count):
            lat = jnp.clip(first + i, 0, NLAT - 1)
            at = pl.ds(pl.multiple_of(lat * NLON, NLON), NLON)
            s_wd[i : i + 1, :] = wd[sub : sub + 1, at]
            s_ws[i : i + 1, :] = ws[sub : sub + 1, at]
            s_k[i : i + 1, :] = jnp.full((1, LANES), diff[lat], F32)
        size = -(-count // 8) * 8
        speed, way, k = s_ws[:size, :], s_wd[:size, :], s_k[:size, :]
        u = v = jnp.zeros((size, LANES), F32)
        for c in range(table.shape[1]):
            u = jnp.where(speed == c, table[0, c], u)
            v = jnp.where(speed == c, table[1, c], v)
        lat = first + lax.broadcasted_iota(jnp.int32, (size, LANES), 0)
        keep = jnp.logical_and(lat >= 0, lat < NLAT)
        u, v, k = (jnp.where(keep, x, 0.0) for x in (u, v, k))
        whole = jnp.where(keep, 1.0 - 4.0 * k, 0.0)
        return jnp.where((way & 1) == 0, u, -u), jnp.where(way < 2, v, -v), k, whole

    lat_row = lax.axis_index("row") * rows
    lat_col = lax.axis_index("col") * cols
    count = rows + 5
    x0, y0, _, _ = parts(lat_row - 4, count, 0)
    x1, y1, _, _ = parts(lat_row - 5, count, 1)
    _, _, k, whole = parts(lat_row - 4, count, 1)
    kr[0, : k.shape[0], :] = k
    kr[1, : k.shape[0], :] = whole
    tile[...] = jnp.zeros_like(tile)
    for g in range(wr.shape[0]):
        n = min(32, k.shape[0] - 32 * g)
        for a, x in enumerate((x0, y0, x1, y1)):
            tile[32 * a : 32 * a + n, :] = x[32 * g : 32 * g + n, :]
        wr[g] = tile[...].T
    for sub in range(2):
        x, y, k, whole = parts(lat_col - 1, cols + 2, sub)
        for a, o in enumerate(five(x, y, k, whole)):
            wc[5 * sub + a, : o.shape[0], :] = o


def five(x, y, k, whole):
    none = jnp.zeros_like(x)
    return (
        whole - jnp.abs(x) - jnp.abs(y),
        jnp.maximum(x, none) + k,
        k - jnp.minimum(x, none),
        jnp.maximum(y, none) + k,
        k - jnp.minimum(y, none),
    )


def weights_call(rows, cols, wd, ws, table, diff):
    most = -(-(max(rows, cols) + 5) // 8) * 8
    groups = -(-(rows + 5) // 32)
    smem = pl.BlockSpec(memory_space=pltpu.SMEM)
    vmem = pl.BlockSpec(memory_space=pltpu.VMEM)
    return pl.pallas_call(
        functools.partial(weights_kernel, rows, cols),
        in_specs=[vmem, vmem, smem, smem],
        out_specs=[vmem, vmem, vmem],
        out_shape=[
            jax.ShapeDtypeStruct((groups, NLON, LANES), F32),
            jax.ShapeDtypeStruct((2, -(-(rows + 5) // 8) * 8, LANES), F32),
            jax.ShapeDtypeStruct((10, -(-(cols + 2) // 8) * 8, LANES), F32),
        ],
        scratch_shapes=[
            pltpu.VMEM((most, LANES), jnp.int32),
            pltpu.VMEM((most, LANES), jnp.int32),
            pltpu.VMEM((most, LANES), F32),
            pltpu.VMEM((LANES, LANES), F32),
        ],
        compiler_params=params(),
        cost_estimate=cost(100000, 1 << 23),
    )(wd, ws, table, diff)


def lane_weights(wr, kr, index, row, sub, height=8):
    w = wr[(index + 1) // 32, pl.ds(row, height), :]
    if isinstance(index, int):
        lane = [32 * (2 * sub + a) + (index + 1) % 32 for a in range(2)]
    else:
        w = pltpu.roll(w, LANES - lax.rem(index + 1, 32), 1)
        lane = [32 * (2 * sub + a) for a in range(2)]
    x, y = (jnp.broadcast_to(w[:, a : a + 1], (height, LANES)) for a in lane)
    k, whole = (jnp.broadcast_to(kr[a, pl.ds(index + 1 - sub, 1), :], (height, LANES)) for a in range(2))
    return five(x, y, k, whole)


def lay_out(wr, kr, index, row, W, subs=(0, 1)):
    for sub in subs:
        for k, x in enumerate(lane_weights(wr, kr, index, row, sub)):
            W[5 * sub + k, pl.ds(row, 8), :] = x


def edge_kernel(pieces, runs, waits, n_refs, rims, wr, kr, *refs):
    sources, to = refs[:n_refs], refs[n_refs : n_refs + 2]
    if rims:
        rim_to, rim_vmem, rim_sem, refs = refs[n_refs + 2 : n_refs + 4], refs[-3:-1], refs[-1], refs[:-3]
    (left, right), f, g, W, sem, sent = refs[-14:-12], refs[-12:-8], refs[-8:-4], refs[-4:-2], refs[-2], refs[-1]
    sub_row = lax.broadcasted_iota(jnp.int32, (8, LANES), 0)
    wide = sources[0].shape[1]
    copies = []
    for i, (ref, row, count, place) in enumerate(pieces):
        for c, lane in enumerate((0, LANES, wide - 2 * LANES, wide - LANES)):
            copies.append(
                pltpu.make_async_copy(
                    sources[ref].at[pl.ds(row, count * 128), pl.ds(lane, LANES)],
                    f[c].at[pl.ds(place * 128, count * 128), :],
                    sem.at[4 * i + c],
                )
            )
    for c in copies:
        c.start()
    if rims:
        height = sources[0].shape[0]
        rim_in = [
            pltpu.make_async_copy(sources[0].at[pl.ds(at, 256), :], rim_vmem[i], rim_sem.at[i])
            for i, at in enumerate((0, height - 256))
        ]
        rim_out = [pltpu.make_async_copy(rim_vmem[i], rim_to[i], rim_sem.at[2 + i]) for i in range(2)]
        for c in rim_in:
            c.start()

    def around(load, j):
        mid = load(8 * j)
        if j == 0:
            west = jnp.where(sub_row == 0, pltpu.roll(load(120), 1, 0), pltpu.roll(mid, 1, 0))
        else:
            west = load(8 * j - 1)
        if j == 15:
            east = jnp.where(sub_row == 7, pltpu.roll(load(0), 7, 0), pltpu.roll(mid, 7, 0))
        else:
            east = load(8 * j + 1)
        return mid, west, east

    def apply(src, base, index, sub, par, store):
        for j in range(16):
            lay_out(wr, kr, index + 1, 8 * j, W[1 - par], (sub,))
            w = [W[par][5 * sub + k, 8 * j : 8 * j + 8, :] for k in range(5)]
            for c in range(4):
                mid, west, east = around(lambda r: src[c][pl.ds(base + 128 + r, 8), :], j)
                so, no = src[c][pl.ds(base + 8 * j, 8), :], src[c][pl.ds(base + 256 + 8 * j, 8), :]
                store(c, 8 * j, w[0] * mid + w[1] * west + w[2] * east + w[3] * so + w[4] * no)

    def to_g(base, place, first, i, par):
        def store(c, r, x):
            g[c][pl.ds(base + r, 8), :] = x

        apply(f, pl.multiple_of(place * 128 + i * 128, 128), first + i + 2, 0, par, store)

    def to_out(base, first, i, at, par):
        def store(c, r, x):
            out = (left, right)[c // 2]
            out[pl.ds(at + r, 8), (c % 2) * LANES : (c % 2 + 1) * LANES] = x

        apply(g, base, first + i + 4, 1, par, store)

    out = []
    for run, (place, at, first, count) in enumerate(runs):
        for j in range(16):
            lay_out(wr, kr, first + 2, 8 * j, W[0], (0,))
            lay_out(wr, kr, first + 4, 8 * j, W[0], (1,))
        done = 0
        for chunk, size in enumerate(chunks(count)):
            for p in waits[run][chunk]:
                for c in copies[4 * p : 4 * p + 4]:
                    c.wait()
            g_first = done + 2 if done else 0

            @pl.loop(g_first // 2, (done + size + 2) // 2)
            def _(i):
                for par in range(2):
                    to_g(pl.multiple_of((2 * i + par) * 128, 128), place, first, 2 * i + par, par)

            @pl.loop(done // 2, (done + size) // 2)
            def _(i):
                for par in range(2):
                    k = 2 * i + par
                    to_out(pl.multiple_of(k * 128, 128), first, k, pl.multiple_of(at * 128 + k * 128, 128), par)

            rows = pl.ds((at + done) * 128, size * 128)
            for i, (a, b) in enumerate(((left, to[0]), (right, to[1]))):
                out.append(pltpu.make_async_copy(a.at[rows, :], b.at[rows, :], sent.at[len(out)]))
                out[-1].start()
            done += size
            if rims and chunk == 0:
                for c, d in zip(rim_in, rim_out):
                    c.wait()
                    d.start()
    for c in out + (rim_out if rims else []):
        c.wait()


def chunks(count):
    return [8] * (count // 8) + ([count % 8] if count % 8 else [])


def edge_call(sources, wr, kr, pieces, runs, waits, later=(), rims=False):
    size = max(p + c for _, _, c, p in pieces)
    count = sum(r[3] for r in runs)
    out = jax.ShapeDtypeStruct((count * 128, 2 * LANES), F32)
    vmem = pl.BlockSpec(memory_space=pltpu.VMEM)
    n = sum(len(chunks(r[3])) for r in runs)
    rim = jax.ShapeDtypeStruct((256, sources[0].shape[1]), F32)
    return pl.pallas_call(
        functools.partial(edge_kernel, pieces, runs, waits, len(sources) + len(later), rims),
        in_specs=[vmem, vmem] + [vmem if x.shape[0] == 256 else ANY for x in sources] + [ANY] * len(later),
        out_specs=[ANY] * (4 if rims else 2),
        out_shape=[out, out] + ([rim, rim] if rims else []),
        scratch_shapes=[pltpu.VMEM(out.shape, F32)] * 2
        + [pltpu.VMEM((size * 128, LANES), F32)] * 4
        + [pltpu.VMEM((max(r[3] for r in runs) * 128 + 256, LANES), F32)] * 4
        + [pltpu.VMEM((10, 128, LANES), F32)] * 2
        + [pltpu.SemaphoreType.DMA((4 * len(pieces),)), pltpu.SemaphoreType.DMA((2 * n,))]
        + ([pltpu.VMEM(rim.shape, F32)] * 2 + [pltpu.SemaphoreType.DMA((4,))] if rims else []),
        compiler_params=params(),
        cost_estimate=cost(count * 128 * 512 * 18, count * 128 * 512 * 8),
    )(wr, kr, *sources, *later)


def roll(x, k):
    return pltpu.roll(x, k, 1)


def one_lat(tiles, slot, mode, index, f_ref, f_base, o_ref, o_base, next_weights, kr, wc, F, G, W, H):
    Fs, F1, F2 = F[slot], F[(slot - 1) % 4], F[(slot - 2) % 4]
    G1, G2, G3 = G[(slot - 1) % 4], G[(slot - 2) % 4], G[(slot - 3) % 4]
    here, after = W[slot % 2], W[(slot + 1) % 2]

    @pl.loop(0, 16 // GROUPS)
    def _(j):
        rs = [pl.multiple_of(j * 8 * GROUPS + 8 * i, 8) for i in range(GROUPS)]
        for r in rs:
            w, lane = next_weights(r)
            for a in range(4):
                after[a, pl.ds(r, 8), :] = jnp.broadcast_to(w[:, 32 * a + lane : 32 * a + lane + 1], (8, LANES))

        def weights(sub, rs):
            k, whole = (jnp.broadcast_to(kr[a, pl.ds(index + 1 - sub, 1), :], (8, LANES)) for a in range(2))
            return [five(here[2 * sub, pl.ds(r, 8), :], here[2 * sub + 1, pl.ds(r, 8), :], k, whole) for r in rs]

        def first(c, rs, w0):
            out = []
            for i, r in enumerate(rs):
                x = f_ref[pl.ds(f_base + r, 8), c * LANES : (c + 1) * LANES]
                Fs[c, pl.ds(PAD + r, 8), :] = x
                if mode >= 1:
                    w = w0[i]
                    g = (
                        w[0] * F1[c, pl.ds(PAD + r, 8), :]
                        + w[1] * F1[c, pl.ds(PAD - 1 + r, 8), :]
                        + w[2] * F1[c, pl.ds(PAD + 1 + r, 8), :]
                        + w[3] * F2[c, pl.ds(PAD + r, 8), :]
                        + w[4] * x
                    )
                    G1[c, pl.ds(PAD + r, 8), :] = g
                    out.append(g)
            return out

        def second(c, rs, w0, w1):
            g = first(c, rs, w0)
            return [
                w[0] * G2[c, pl.ds(PAD + r, 8), :]
                + w[1] * G2[c, pl.ds(PAD - 1 + r, 8), :]
                + w[2] * G2[c, pl.ds(PAD + 1 + r, 8), :]
                + w[3] * G3[c, pl.ds(PAD + r, 8), :]
                + w[4] * g[i]
                for i, (r, w) in enumerate(zip(rs, w1))
            ]

        def across(sub, c, mid, so, no):
            W = [jnp.broadcast_to(wc[5 * sub + k, c + 1 : c + 2, :], (8, LANES)) for k in range(5)]
            out = []
            for i in range(GROUPS):
                t = None
                if mid is not None:
                    t = W[0] * mid[i] + W[1] * roll(mid[i], 1) + W[2] * roll(mid[i], LANES - 1)
                if so is not None:
                    t = W[3] * so[i] if t is None else t + W[3] * so[i]
                if no is not None:
                    t = W[4] * no[i] if t is None else t + W[4] * no[i]
                out.append(t)
            return out

        for part in range(0, GROUPS, PART):
            some = rs[part : part + PART]
            w0 = weights(0, some) if mode >= 1 else None
            w1 = weights(1, some) if mode >= 2 else None
            for c in range(tiles):
                if mode < 2:
                    first(c, some, w0)
                    continue
                for i, x in enumerate(second(c, some, w0, w1)):
                    H[c, 8 * (part + i) : 8 * (part + i) + 8, :] = x
        if mode < 2:
            return
        h, u = {-2: None, -1: None}, {-2: None}
        for c in range(tiles + 2):
            h[c] = [H[c, 8 * i : 8 * i + 8, :] for i in range(GROUPS)] if c < tiles else None
            u[c - 1] = across(0, c - 1, h[c - 1], h[c - 2], h[c])
            if c >= 2:
                o = across(1, c - 2, u[c - 2], u[c - 3], u[c - 1])
                for i, r in enumerate(rs):
                    o_ref[pl.ds(o_base + r, 8), (c - 2) * LANES : (c - 1) * LANES] = o[i]

    for ring in (Fs, G1) if mode >= 1 else (Fs,):
        ring[:, PAD - 1 : PAD, :] = ring[:, PAD + 127 : PAD + 128, :]
        ring[:, PAD + 128 : PAD + 129, :] = ring[:, PAD : PAD + 1, :]


def main_kernel(tiles, wr, kr, wc, f_ref, o_ref, done, *ring):
    F, G, W, H, turned = ring[:4], ring[4:8], ring[8:10], ring[10], ring[11]
    t = pl.program_id(0)
    turned[...] = pltpu.roll(wr[(4 * t + 4) // 32], LANES - lax.rem(4 * t + 4, 32), 1)

    def four(modes):
        for q in range(4):
            next_weights = lambda r, q=q: (turned[pl.ds(r, 8), :], q)
            one_lat(tiles, q, modes[q], 4 * t + q + 2, f_ref, 128 * q, o_ref, 128 * q, next_weights, kr, wc, F, G, W, H)

    done[...] = jnp.zeros_like(done)
    pl.when(t == 0)(lambda: four((0, 0, 1, 1)))
    pl.when(t > 0)(lambda: four((2, 2, 2, 2)))


def rings(tiles):
    return [pltpu.VMEM((tiles, 128 + 2 * PAD, LANES), F32)] * 8 + [pltpu.VMEM((4, 128, LANES), F32)] * 2 + [pltpu.VMEM((tiles, 8 * GROUPS, LANES), F32)]


def main_call(cov, wr, kr, wc):
    rows, wide = cov.shape[0] // 128, cov.shape[1]
    return pl.pallas_call(
        functools.partial(main_kernel, wide // LANES),
        grid=(rows // 4,),
        in_specs=[
            *[pl.BlockSpec(w.shape, lambda s: (0, 0, 0)) for w in (wr, kr, wc)],
            pl.BlockSpec((512, wide), lambda s: (s, 0)),
        ],
        out_specs=[
            pl.BlockSpec((pl.Element(512), pl.Element(wide)), lambda s: (128 * jnp.maximum(4 * s - 2, 2), 0)),
            pl.BlockSpec((8, LANES), lambda s: (0, 0)),
        ],
        out_shape=[jax.ShapeDtypeStruct(cov.shape, F32), jax.ShapeDtypeStruct((8, LANES), F32)],
        scratch_shapes=rings(wide // LANES) + [pltpu.VMEM((128, LANES), F32)],
        compiler_params=params(),
        cost_estimate=cost(cov.size * 36, cov.size * 8),
    )(wr, kr, wc, cov)


def add_halo(tiles, wc, side, halo, e_ref):
    edge, way = (0, 3) if side == 0 else (tiles - 1, 4)
    outer, inner = (-1, 1) if side == 0 else (tiles, tiles - 2)
    near, far = (LANES, 0) if side == 0 else (0, LANES)
    at_edge, at_inner = (0, LANES) if side == 0 else (LANES, 0)

    def weight(sub, k, lat):
        return jnp.broadcast_to(wc[5 * sub + k, lat + 1 : lat + 2, :], (8, LANES))

    a = [weight(0, k, outer) for k in (0, 1, 2, way)]
    b = weight(0, way, edge)
    d = [weight(1, k, edge) for k in (0, 1, 2, way)]
    d = [d[0] * b, d[1] * roll(b, 1), d[2] * roll(b, LANES - 1), d[3]]
    e = weight(1, way, inner) * b

    @pl.loop(0, halo.shape[0] // 128)
    def _(i):
        for j in range(16):
            at = pl.ds(pl.multiple_of(i * 128 + 8 * j, 8), 8)
            f1, f2 = halo[at, near : near + LANES], halo[at, far : far + LANES]
            f_west, f_east = roll(f1, 1), roll(f1, LANES - 1)
            u1 = a[0] * f1 + a[3] * f2 + a[1] * f_west + a[2] * f_east
            e_ref[at, at_edge : at_edge + LANES] = e_ref[at, at_edge : at_edge + LANES] + (
                d[0] * f1 + d[1] * f_west + d[2] * f_east + d[3] * u1
            )
            e_ref[at, at_inner : at_inner + LANES] = e_ref[at, at_inner : at_inner + LANES] + e * f1


class Copies:
    def __init__(self, sem):
        self.sem, self.n = sem, 0

    def start(self, src, dst):
        c = pltpu.make_async_copy(src, dst, self.sem.at[self.n])
        self.n += 1
        c.start()
        return c


def tail_kernel(tiles, rows, wr, kr, wc, before, after, low, high, cov, o_in, o_hbm, *scratch):
    halo, own, rim, side_halo, side_own = (scratch[2 * i : 2 * i + 2] for i in range(5))
    F, G, W, H, sem = scratch[10:14], scratch[14:18], scratch[18:20], scratch[20], scratch[21]
    copies = Copies(sem)
    wide, size = tiles * LANES, (rows - 4) * 128
    inside = pl.ds(256, size)
    lanes = [pl.ds(0, 256), pl.ds(wide - 256, 256)]

    def bring(i):
        if i < 2:
            x = (before, after)[i]
            return [copies.start(x, halo[i]), copies.start(cov.at[pl.ds(i * (rows - 4) * 128, 512), :], own[i])]
        x = (low, high)[i - 2]
        return [copies.start(x, side_halo[i - 2]), copies.start(o_in.at[inside, lanes[i - 2]], side_own[i - 2])]

    ins, out = [bring(0)], []
    for i in range(2):
        for c in ins[i]:
            c.wait()
        ins += [bring(1), bring(2)] if i == 0 else [bring(3)]
        mine, theirs = [(own[i], 128 * q) for q in range(4)], [(halo[i], 128 * q) for q in range(2)]
        index = (rows - 2) * i
        for q, (mode, (ref, base)) in enumerate(zip((0, 0, 1, 1, 2, 2), mine + theirs if i else theirs + mine)):
            at = index + q + 2
            next_weights = lambda r, at=at: (wr[at // 32, pl.ds(r, 8), :], at % 32)
            one_lat(tiles, q % 4, mode, index + q, ref, base, rim[i], 128 * (q - 4), next_weights, kr, wc, F, G, W, H)
        out.append(copies.start(rim[i], o_hbm.at[pl.ds(i * (rows - 2) * 128, 256), :]))
    for i in range(2):
        for c in ins[2 + i]:
            c.wait()
        add_halo(tiles, wc, i, side_halo[i], side_own[i])
        out.append(copies.start(side_own[i], o_hbm.at[inside, lanes[i]]))
    for c in out:
        c.wait()


def tail_call(cov, wr, kr, wc, before, after, low, high, out):
    rows, wide = cov.shape[0] // 128, cov.shape[1]
    vmem = pl.BlockSpec(memory_space=pltpu.VMEM)
    return pl.pallas_call(
        functools.partial(tail_kernel, wide // LANES, rows),
        in_specs=[vmem] * 3 + [ANY] * 6,
        out_specs=ANY,
        out_shape=jax.ShapeDtypeStruct(cov.shape, F32),
        scratch_shapes=[pltpu.VMEM((256, wide), F32)] * 2
        + [pltpu.VMEM((512, wide), F32)] * 2
        + [pltpu.VMEM((256, wide), F32)] * 2
        + [pltpu.VMEM(low.shape, F32)] * 4
        + rings(wide // LANES)
        + [pltpu.SemaphoreType.DMA((12,))],
        input_output_aliases={8: 0},
        compiler_params=params(),
        cost_estimate=cost(cov.size * 8, cov.size * 3),
    )(wr, kr, wc, before, after, low, high, cov, out)


def corner_kernel(tiles, rows, wc, low, high, o_in, o_hbm, own0, own1, halo0, halo1, sem):
    copies = Copies(sem)
    wide = tiles * LANES
    parts = [(i, pl.ds(256 * i, 256), pl.ds(i * (rows - 2) * 128, 256)) for i in range(2)]
    lanes = [pl.ds(0, 256), pl.ds(wide - 256, 256)]
    own = (own0, own1)
    ins = [[copies.start(o_in.at[there, lanes[s]], own[s].at[here, :]) for _, here, there in parts] for s in range(2)]
    for s, (x, halo) in enumerate(((low, halo0), (high, halo1))):
        ins[s].append(copies.start(x, halo))
    out = []
    for s, halo in enumerate((halo0, halo1)):
        for c in ins[s]:
            c.wait()
        add_halo(tiles, wc, s, halo, own[s])
        out += [copies.start(own[s].at[here, :], o_hbm.at[there, lanes[s]]) for _, here, there in parts]
    for c in out:
        c.wait()


def corner_call(wc, low, high, out):
    rows, wide = out.shape[0] // 128, out.shape[1]
    vmem = pl.BlockSpec(memory_space=pltpu.VMEM)
    return pl.pallas_call(
        functools.partial(corner_kernel, wide // LANES, rows),
        in_specs=[vmem] + [ANY] * 3,
        out_specs=ANY,
        out_shape=jax.ShapeDtypeStruct(out.shape, F32),
        scratch_shapes=[pltpu.VMEM(low.shape, F32)] * 4 + [pltpu.SemaphoreType.DMA((10,))],
        input_output_aliases={3: 0},
        compiler_params=params(),
        cost_estimate=cost(low.size * 20, low.size * 24),
    )(wc, low, high, out)


def local(cov, wind_direction, wind_speed, speed_table, diffusivity):
    rows, tiles = cov.shape[0] // 128, cov.shape[1] // LANES
    n_row, n_col = lax.axis_size("row"), lax.axis_size("col")
    up = lambda n: [(i, i + 1) for i in range(n - 1)]
    down = lambda n: [(i + 1, i) for i in range(n - 1)]
    wr, kr, wc = weights_call(rows, tiles, wind_direction, wind_speed, speed_table, diffusivity)
    sizes = chunks(rows - 4)
    sizes[0] += 4
    starts = [sum(sizes[:i]) for i in range(len(sizes))]
    pieces = [(0, 128 * a, n, a) for a, n in zip(starts, sizes)]
    left, right, first, final = edge_call(
        [cov], wr, kr, pieces, [(0, 0, 2, rows - 4)], [[[i] for i in range(len(sizes))]], rims=True
    )
    before = lax.ppermute(final, "row", up(n_row))
    after = lax.ppermute(first, "row", down(n_row))
    low = lax.ppermute(right, "col", up(n_col))
    high = lax.ppermute(left, "col", down(n_col))
    out, done = main_call(cov, wr, kr, wc)
    left, right = edge_call(
        [before, cov, after],
        wr,
        kr,
        [(0, 0, 2, 0), (1, 0, 4, 2), (1, 128 * (rows - 4), 4, 6), (2, 0, 2, 10)],
        [(0, 0, 0, 2), (6, 2, rows - 2, 2)],
        [[[0, 1]], [[2, 3]]],
        [done],
    )
    low_c = lax.ppermute(right, "col", up(n_col))
    high_c = lax.ppermute(left, "col", down(n_col))
    out = tail_call(cov, wr, kr, wc, before, after, low, high, out)
    return corner_call(wc, low_c, high_c, out)


def solution(mesh):
    return jax.shard_map(
        local,
        mesh=mesh,
        in_specs=(P("row", "col"), P(), P(), P(), P()),
        out_specs=P("row", "col"),
        check_vma=False,
    )
```
